256 devices in a mesh: space: 8 (over x_hi, y), tm: 32 (over x_lo, z, core).
Axes of the slice: x: 4 (x_hi: 2, x_lo: 2; x = x_hi * 2 + x_lo), y: 4, z: 8, core: 2. Of those that a mesh axis runs over, the one named last changes fastest.
Arguments:
- fields: float32 [16384, 32768], P('space', 'tm'), may hold values from -6 to 6
- range_test: float32 [32768, 64], P('tm'), may hold values from -0.03125 to 0.03125
- corange_test: float32 [128, 16384], P(None, 'space'), may hold values from -0.0625 to 0.0625
- core_left: float32 [256, 16384], P(None, 'space'), may hold values from -0.0625 to 0.0625
- core_right: float32 [256, 32768], P(None, 'tm'), may hold values from -0.0625 to 0.0625
Outputs:
- range_sketch: float32 [16384, 64], P('space')
- corange_sketch: float32 [128, 32768], P('space', 'tm')
- core_sketch: float32 [256, 256], P('space', 'tm')
The draws below stay inside these ranges and needn't reach their ends.
All inputs are finite; a program needn't handle non-finite values.
Results may differ from the reference program's by a relative error of at most 0.000073.
Values sent between devices are 32-bit elements; how exact they have to be, the bound alone decides.
A program may use at most 64 MiB of HBM per device.

```python
import jax
import jax.numpy as jnp
from jax import lax

K = 64
L = 128
S = 256
CELLS = 16384
SNAPS = 32768


def strengthened(result, own_key, source, target, shards_of, factor):
    def block_of(dim):
        return (jnp.arange(result.shape[dim]) // (result.shape[dim] // shards_of)).reshape((-1,) + (1,) * (result.ndim - 1 - dim))

    first = jax.random.permutation(own_key, shards_of)[block_of(target)]
    second = (block_of(target) + shards_of // 2) % shards_of
    return jnp.where((block_of(source) == first) | (block_of(source) == second), factor * result, result)


def steps_of(rng, shape, pieces, least, high):
    level = 1.0
    for position, blocks in pieces:
        steps = jax.random.uniform(jax.random.fold_in(jax.random.fold_in(rng, 6), position), (blocks,), jnp.float32, least / len(pieces), high / len(pieces))
        level = level * jnp.repeat(jnp.exp(steps), shape[position] // blocks).reshape((-1,) + (1,) * (len(shape) - 1 - position))
    return level


def noise(stream_key, shape, spread, reach, split=(), dtype=jnp.bfloat16):
    values = spread * jax.random.normal(stream_key, shape, jnp.float32)
    if split:
        values = values * steps_of(stream_key, shape, split, -0.22, 0.18)
    return jnp.clip(values, -reach, reach).astype(dtype)


def bell_draw_with(key, shape, spread, most, split, heavy, kind=jnp.bfloat16):
    entries = spread * jax.random.normal(key, shape, jnp.float32)
    if split:
        entries = entries * steps_of(key, shape, split, -0.22, 0.18)
    return jnp.clip(strengthened(entries, jax.random.fold_in(key, 3), *heavy), -most, most).astype(kind)


def setup_inputs(seed: int = 0) -> dict:
    arg_keys = jax.random.split(jax.random.key(seed), 6)
    return {
        "fields": noise(arg_keys[0], (CELLS, SNAPS), 1.0, 6.0, ((0, 8), (1, 32)), jnp.float32),
        "range_test": noise(arg_keys[1], (SNAPS, K), SNAPS ** -0.5, 0.03125, ((0, 32),), jnp.float32),
        "corange_test": bell_draw_with(arg_keys[2], (L, CELLS), CELLS ** -0.5, 0.0625, ((1, 8),), (1, 0, 8, 2.0), jnp.float32),
        "core_left": bell_draw_with(arg_keys[3], (S, CELLS), CELLS ** -0.5, 0.0625, ((1, 8),), (1, 0, 8, 2.0), jnp.float32),
        "core_right": bell_draw_with(arg_keys[4], (S, SNAPS), SNAPS ** -0.5, 0.0625, ((1, 32),), (1, 0, 32, 2.75), jnp.float32),
    }


def reference(fields, range_test, corange_test, core_left, core_right):
    highest = lax.Precision.HIGHEST
    range_sketch = jnp.dot(fields, range_test, precision=highest, preferred_element_type=jnp.float32)
    corange_sketch = jnp.dot(corange_test, fields, precision=highest, preferred_element_type=jnp.float32)
    mixed = jnp.dot(core_left, fields, precision=highest, preferred_element_type=jnp.float32)
    core_sketch = jnp.dot(mixed, core_right.T, precision=highest, preferred_element_type=jnp.float32)
    return (range_sketch, corange_sketch, core_sketch)
```

```python
import jax
import jax.numpy as jnp
from jax import lax
from jax.experimental import pallas as pl
from jax.experimental.pallas import tpu as pltpu
from jax.sharding import PartitionSpec as P

MESH = pl.DeviceIdType.MESH
F32, BF16 = jnp.float32, jnp.bfloat16
NN = (((1,), (0,)), ((), ()))
NT = (((1,), (1,)), ((), ()))
XH, Y, XL, Z, C = 2, 4, 2, 8, 2
CHUNK = 256
PLANE = [(i, j, k) for i in range(XH) for j in range(Y) for k in range(XL) if i or j or k]
COLUMN = [(i, j) for i in range(Z) for j in range(C) if i or j]
SPACE = [(i, j) for i in range(XH) for j in range(Y) if i or j]


def dot(a, b, dims):
    return lax.dot_general(a, b, dims, preferred_element_type=F32)


def split(x):
    high = x.astype(BF16)
    return high, (x - high.astype(F32)).astype(BF16)


def kernel(
    f_hbm, r_hbm, a_hbm, l_hbm, q_hbm,
    range_ref, corange_ref, core_ref,
    f, r, a, l, q, fh, fl, rr, ah, aa, lh, ll, qh, ql,
    rp, rc, rx, rs, rz,
    cp, ca, mp, ma, mb, mc,
    load_f, load, core_s, core_r, x_s, x_r, z_s, z_r, ag_s, ag_r, xg_s, xg_r, cg_s, cg_r,
    c_s, c_r, ma_s, ma_r, mb_s, mb_r,
):
    s, t = lax.axis_index("space"), lax.axis_index("tm")
    xh, y = s // Y, s % Y
    xl, z, c = t // (Z * C), (t // C) % Z, t % C

    def at(dxh=0, dy=0, dxl=0, dz=0, dc=0):
        return (
            lax.rem(xh + dxh, XH) * Y + lax.rem(y + dy, Y),
            lax.rem(xl + dxl, XL) * (Z * C) + lax.rem(z + dz, Z) * C + lax.rem(c + dc, C),
        )

    def remote(src, dst, ss, rs_, **where):
        return pltpu.make_async_remote_copy(
            src_ref=src, dst_ref=dst, send_sem=ss, recv_sem=rs_, device_id=at(**where), device_id_type=MESH
        )

    n_chunks = f.shape[0]
    half = n_chunks // C
    other = lax.rem(c + 1, C)
    xo = lax.rem(xl + 1, XL)

    loads = [pltpu.make_async_copy(src, dst, load.at[i]) for i, (src, dst) in enumerate(((r_hbm, r), (l_hbm, l), (q_hbm, q), (a_hbm, a)))]

    def f_load(chunk):
        rows = pl.ds(pl.multiple_of(chunk * CHUNK, CHUNK), CHUNK)
        return pltpu.make_async_copy(f_hbm.at[rows, :], f.at[chunk], load_f.at[chunk])

    loads[0].start()
    for k in range(half):
        f_load(other * half + k).start()
    for k in range(half):
        f_load(c * half + k).start()
    for cp_ in loads[1:]:
        cp_.start()

    barrier = pltpu.get_barrier_semaphore()
    for i, j, k in PLANE:
        pl.semaphore_signal(barrier, inc=1, device_id=at(dxh=i, dy=j, dxl=k), device_id_type=MESH)
    for i, j in COLUMN:
        pl.semaphore_signal(barrier, inc=1, device_id=at(dz=i, dc=j), device_id_type=MESH)

    loads[0].wait()
    high, low = split(r[...])
    kk = high.shape[0]
    rr[:kk, :] = high
    rr[kk:, :] = low

    def range_chunk(chunk):
        f_load(chunk).wait()
        high, low = split(f[chunk])
        rows = pl.ds(pl.multiple_of(chunk * CHUNK, CHUNK), CHUNK)
        fh[rows, :] = high
        fl[rows, :] = low
        both = dot(rr[...], high, NT)
        out = both[:kk] + both[kk:] + dot(rr[:kk, :], low, NT)
        rp[2 * chunk] = out[:, :128]
        rp[2 * chunk + 1] = out[:, 128:]

    @pl.loop(0, half)
    def _(k):
        range_chunk(other * half + k)

    pl.semaphore_wait(barrier, len(PLANE) + len(COLUMN))

    def core_copy(k):
        return remote(rp.at[pl.ds(other * Z + 2 * k, 2)], rc.at[pl.ds(2 * k, 2)], core_s.at[k], core_r.at[k], dc=1)

    for k in range(half):
        core_copy(k).start()

    krows = kk // XL
    mine = pl.ds(pl.multiple_of(xl * krows, krows), krows)
    theirs = pl.ds(pl.multiple_of(xo * krows, krows), krows)

    def x_copy(k):
        return remote(
            rp.at[pl.ds(c * Z + 2 * k, 2), theirs], rx.at[pl.ds(2 * k, 2)], x_s.at[k], x_r.at[k], dxl=1
        )

    @pl.loop(0, half)
    def _(k):
        range_chunk(c * half + k)
        core_copy(k).wait_recv()
        own = pl.ds(c * Z + 2 * k, 2)
        rp[own] = rp[own] + rc[pl.ds(2 * k, 2)]
        x_copy(k).start()

    loads[1].wait()
    high, low = split(l[...])
    m_rows = high.shape[0]
    lh[...] = high
    ll[...] = low
    loads[2].wait()
    high, low = split(q[...])
    qh[...] = high
    ql[...] = low

    def mixed_chunk(j):
        cols = slice(j * CHUNK, (j + 1) * CHUNK)
        m = dot(lh[...], fh[:, cols], NN) + dot(ll[...], fh[:, cols], NN) + dot(lh[...], fl[:, cols], NN)
        mh, ml = split(m)
        return dot(mh, qh[:, cols], NT) + dot(ml, qh[:, cols], NT) + dot(mh, ql[:, cols], NT)

    n_cols = fh.shape[1] // CHUNK
    total = mixed_chunk(0)

    def z_copy(d):
        return remote(rs.at[lax.rem(z + d, Z)], rz.at[d - 1], z_s.at[d - 1], z_r.at[d - 1], dz=d)

    for j in range(1, n_cols):
        total = total + mixed_chunk(j)
        if j == 1:
            for k in range(half):
                x_copy(k).wait_recv()
                rs[pl.ds(2 * k, 2)] = rp[pl.ds(c * Z + 2 * k, 2), mine] + rx[pl.ds(2 * k, 2)]
            for d in range(1, Z):
                z_copy(d).start()

    rows = m_rows // (XH * Y)
    for i in range(XH * Y):
        for k in range(XL):
            mp[i, k] = total[i * rows : (i + 1) * rows, k * 128 : (k + 1) * 128]

    def ma_copy(n):
        i, j, k = PLANE[n]
        to = lax.rem(xh + i, XH) * Y + lax.rem(y + j, Y)
        return remote(mp.at[to, lax.rem(xl + k, XL)], ma.at[n], ma_s.at[n], ma_r.at[n], dxh=i, dy=j, dxl=k)

    for n in range(len(PLANE)):
        ma_copy(n).start()

    loads[3].wait()
    high, low = split(a[...])
    c_rows = high.shape[0]
    aa[:c_rows, :] = high
    aa[c_rows:, :] = low
    piece = c_rows // (XH * Y)

    def c_copy(n, j):
        dxh, dy = SPACE[n]
        to = lax.rem(xh + dxh, XH) * Y + lax.rem(y + dy, Y)
        return remote(cp.at[j, to], ca.at[j, n], c_s.at[j, n], c_r.at[j, n], dxh=dxh, dy=dy)

    for j in range(n_cols):
        cols = slice(j * CHUNK, (j + 1) * CHUNK)
        both = dot(aa[...], fh[:, cols], NN)
        out = both[:c_rows] + both[c_rows:] + dot(aa[:c_rows, :], fl[:, cols], NN)
        for i in range(XH * Y):
            cp[j, i] = out[i * piece : (i + 1) * piece]
        for n in range(len(SPACE)):
            c_copy(n, j).start()

    for d in range(1, Z):
        z_copy(d).wait_recv()
    done = rs[z]
    for d in range(1, Z):
        done = done + rz[d - 1]

    def spot(zz, rows_):
        return range_ref.at[rows_, pl.ds(pl.multiple_of((c * Z + zz) * 128, 128), 128)]

    own_piece = spot(z, mine)
    own_piece[...] = done

    def ag_copy(d):
        return remote(own_piece, own_piece, ag_s.at[d - 1], ag_r.at[d - 1], dz=d)

    for d in range(1, Z):
        ag_copy(d).start()

    def ag_arrival(d):
        there = spot(lax.rem(z + Z - d, Z), mine)
        return remote(there, there, ag_s.at[d - 1], ag_r.at[d - 1], dz=d)

    def xg_copy(d):
        there = spot(lax.rem(z + Z - d, Z), mine)
        return remote(there, there, xg_s.at[d], xg_r.at[d], dxl=1)

    def xg_arrival(d):
        there = spot(lax.rem(z + Z - d, Z), theirs)
        return remote(there, there, xg_s.at[d], xg_r.at[d], dxl=1)

    def cg_copy(d, k):
        there = spot(lax.rem(z + Z - d, Z), (mine, theirs)[k])
        return remote(there, there, cg_s.at[k, d], cg_r.at[k, d], dc=1)

    def cg_arrival(d, k):
        zz = lax.rem(z + Z - d, Z)
        cols_ = pl.ds(pl.multiple_of((other * Z + zz) * 128, 128), 128)
        there = range_ref.at[(mine, theirs)[k], cols_]
        return remote(there, there, cg_s.at[k, d], cg_r.at[k, d], dc=1)

    xg_copy(0).start()
    cg_copy(0, 0).start()

    for n in range(len(PLANE)):
        ma_copy(n).wait_recv()
    block = mp[s, xl]
    for n in range(len(PLANE)):
        block = block + ma[n]
    block = jnp.concatenate([block, jnp.zeros((128 - rows, 128), F32)], 0).T
    for i in range(Z * C):
        mb[i] = block[8 * i : 8 * i + 8]

    def mb_copy(n):
        i, j = COLUMN[n]
        to = lax.rem(z + i, Z) * C + lax.rem(c + j, C)
        return remote(mb.at[to], mc.at[n], mb_s.at[n], mb_r.at[n], dz=i, dc=j)

    for n in range(len(COLUMN)):
        mb_copy(n).start()

    order = [1, 7, 2, 6, 3, 5, 4]
    for d in order:
        ag_arrival(d).wait_recv()
        xg_copy(d).start()
        cg_copy(d, 0).start()
    for d in [0] + order:
        xg_arrival(d).wait_recv()
        cg_copy(d, 1).start()

    for j in range(n_cols):
        for n in range(len(SPACE)):
            c_copy(n, j).wait_recv()
        out = cp[j, s]
        for n in range(len(SPACE)):
            out = out + ca[j, n]
        corange_ref[:, j * CHUNK : (j + 1) * CHUNK] = out

    for n in range(len(COLUMN)):
        mb_copy(n).wait_recv()
    out = mb[z * C + c]
    for n in range(len(COLUMN)):
        out = out + mc[n]
    core_ref[...] = out[:, :rows]

    for d in [0] + order:
        for k in range(2):
            cg_arrival(d, k).wait_recv()

    for k in range(half):
        core_copy(k).wait_send()
        x_copy(k).wait_send()
    for d in range(1, Z):
        z_copy(d).wait_send()
        ag_copy(d).wait_send()
    for d in range(Z):
        xg_copy(d).wait_send()
        for k in range(2):
            cg_copy(d, k).wait_send()
    for n in range(len(PLANE)):
        ma_copy(n).wait_send()
    for n in range(len(COLUMN)):
        mb_copy(n).wait_send()
    for j in range(n_cols):
        for n in range(len(SPACE)):
            c_copy(n, j).wait_send()


def shards(fields, range_test, corange_test, core_left, core_right):
    cells, snaps = fields.shape
    k, l, m = range_test.shape[1], corange_test.shape[0], core_left.shape[0]
    n_cols = snaps // CHUNK
    vmem = pl.BlockSpec(memory_space=pltpu.VMEM)
    dma = pltpu.SemaphoreType.DMA
    v = pltpu.VMEM
    range_t, corange, core_t = pl.pallas_call(
        kernel,
        out_shape=(
            jax.ShapeDtypeStruct((k, cells), F32),
            jax.ShapeDtypeStruct((l // (XH * Y), snaps), F32),
            jax.ShapeDtypeStruct((m // (XL * Z * C), m // (XH * Y)), F32),
        ),
        in_specs=[pl.BlockSpec(memory_space=pl.ANY)] * 5,
        out_specs=(vmem,) * 3,
        scratch_shapes=[
            v((cells // CHUNK, CHUNK, snaps), F32),
            v((k, snaps), F32),
            v((l, cells), F32),
            v((m, cells), F32),
            v((m, snaps), F32),
            v((cells, snaps), BF16),
            v((cells, snaps), BF16),
            v((2 * k, snaps), BF16),
            v((16, 128), BF16),
            v((2 * l, cells), BF16),
            v((m, cells), BF16),
            v((m, cells), BF16),
            v((m, snaps), BF16),
            v((m, snaps), BF16),
            v((Z * C, k, 128), F32),
            v((Z, k, 128), F32),
            v((Z, k // XL, 128), F32),
            v((Z, k // XL, 128), F32),
            v((Z - 1, k // XL, 128), F32),
            v((n_cols, XH * Y, l // (XH * Y), CHUNK), F32),
            v((n_cols, len(SPACE), l // (XH * Y), CHUNK), F32),
            v((XH * Y, XL, m // (XH * Y), 128), F32),
            v((len(PLANE), m // (XH * Y), 128), F32),
            v((Z * C, 8, 128), F32),
            v((len(COLUMN), 8, 128), F32),
            dma((cells // CHUNK,)),
            dma((4,)),
            dma((4,)), dma((4,)),
            dma((4,)), dma((4,)),
            dma((Z - 1,)), dma((Z - 1,)),
            dma((Z - 1,)), dma((Z - 1,)),
            dma((Z,)), dma((Z,)),
            dma((2, Z)), dma((2, Z)),
            dma((n_cols, len(SPACE))), dma((n_cols, len(SPACE))),
            dma((len(PLANE),)), dma((len(PLANE),)),
            dma((len(COLUMN),)), dma((len(COLUMN),)),
        ],
        compiler_params=pltpu.CompilerParams(
            collective_id=0, has_side_effects=True, vmem_limit_bytes=60 << 20
        ),
        name="sketch",
    )(fields, range_test.T, corange_test, core_left, core_right)
    return range_t.T, corange, core_t.T


def solution(mesh):
    placed = (P("space", "tm"), P("tm", None), P(None, "space"), P(None, "space"), P(None, "tm"))
    return jax.shard_map(
        shards,
        mesh=mesh,
        in_specs=placed,
        out_specs=(P("space", None), P("space", "tm"), P("space", "tm")),
        check_vma=False,
    )
```

```python
import jax
import jax.numpy as jnp
from jax import lax
from jax.experimental import pallas as pl
from jax.experimental.pallas import tpu as pltpu
from jax.sharding import PartitionSpec as P

MESH = pl.DeviceIdType.MESH
F32, BF16 = jnp.float32, jnp.bfloat16
NN = (((1,), (0,)), ((), ()))
NT = (((1,), (1,)), ((), ()))
XH, Y, XL, Z, C = 2, 4, 2, 8, 2
CHUNK = 512
WIDTH = 512
PLANE = sorted(
    ((i, j, k) for i in range(XH) for j in range(Y) for k in range(XL) if i or j or k),
    key=lambda p: (-2 * p[0] - min(p[1], Y - p[1]) - p[2], p),
)
COLUMN = sorted(
    ((i, j) for i in range(Z) for j in range(C) if i or j), key=lambda p: (-min(p[0], Z - p[0]), p)
)
ROUND = sorted(
    ((i, k) for i in range(Z) for k in range(XL) if i or k), key=lambda p: (-min(p[0], Z - p[0]) - p[1], p)
)
RING = (2, 1, 3)


def dot(a, b, dims):
    return lax.dot_general(a, b, dims, preferred_element_type=F32)


def split(x):
    high = x.astype(BF16)
    return high, (x - high.astype(F32)).astype(BF16)


def kernel(
    f_hbm, r_hbm, a_hbm, l_hbm, q_hbm,
    range_ref, corange_ref, core_ref,
    f, r, a, l, q, fh, fl, rr, al, qh, ql, mh, ml,
    rp, rc, rz, cp, cy, cs, cx, mp, ma, mb, mc,
    load_f, load, core_s, core_r, z_s, z_r, ag_s, ag_r, xg_s, xg_r, cg_s, cg_r,
    cy_s, cy_r, cx_s, cx_r, ma_s, ma_r, mb_s, mb_r,
):
    s, t = lax.axis_index("space"), lax.axis_index("tm")
    xh, y = s // Y, s % Y
    xl, z, c = t // (Z * C), (t // C) % Z, t % C

    def at(dxh=0, dy=0, dxl=0, dz=0, dc=0):
        return (
            lax.rem(xh + dxh, XH) * Y + lax.rem(y + dy, Y),
            lax.rem(xl + dxl, XL) * (Z * C) + lax.rem(z + dz, Z) * C + lax.rem(c + dc, C),
        )

    def remote(src, dst, ss, rs_, **where):
        return pltpu.make_async_remote_copy(
            src_ref=src, dst_ref=dst, send_sem=ss, recv_sem=rs_, device_id=at(**where), device_id_type=MESH
        )

    def whole(ref, ss, rs_):
        return remote(ref, ref, ss, rs_, dc=1)

    n_chunks = f.shape[0]
    half = n_chunks // C
    groups = CHUNK // 128
    other = lax.rem(c + 1, C)
    xo = lax.rem(xl + 1, XL)

    loads = [
        pltpu.make_async_copy(src, dst, load.at[i])
        for i, (src, dst) in enumerate(((r_hbm, r), (l_hbm, l), (a_hbm, a), (q_hbm, q)))
    ]

    def f_load(chunk):
        rows = pl.ds(pl.multiple_of(chunk * CHUNK, CHUNK), CHUNK)
        return pltpu.make_async_copy(f_hbm.at[rows, :], f.at[chunk], load_f.at[chunk])

    loads[0].start()
    for k in range(half):
        f_load(other * half + k).start()
    for k in range(half):
        f_load(c * half + k).start()
    for cp_ in loads[1:]:
        cp_.start()

    barrier = pltpu.get_barrier_semaphore()
    peers = {(i, j, k, 0, 0) for i, j, k in PLANE} | {(0, 0, 0, i, j) for i, j in COLUMN}
    peers |= {(0, 0, k, i, 0) for i, k in ROUND}

    def far(p):
        return -(2 * p[0] + min(p[1], Y - p[1]) + p[2] + min(p[3], Z - p[3])), p

    for i, j, k, m, n in sorted(peers, key=far):
        pl.semaphore_signal(
            barrier, inc=1, device_id=at(dxh=i, dy=j, dxl=k, dz=m, dc=n), device_id_type=MESH
        )

    loads[0].wait()
    high, low = split(r[...])
    kk = high.shape[0]
    rr[:kk, :] = high
    rr[kk:, :] = low

    def range_chunk(chunk):
        f_load(chunk).wait()
        high, low = split(f[chunk])
        rows = pl.ds(pl.multiple_of(chunk * CHUNK, CHUNK), CHUNK)
        for j in range(fh.shape[0]):
            fh[j, rows, :] = high[:, j * WIDTH : (j + 1) * WIDTH]
            fl[j, rows, :] = low[:, j * WIDTH : (j + 1) * WIDTH]
        both = dot(rr[...], high, NT)
        out = both[:kk] + both[kk:] + dot(rr[:kk, :], low, NT)
        for i in range(groups):
            rp[groups * chunk + i] = out[:, 128 * i : 128 * (i + 1)]

    def core_copy(k):
        return remote(
            rp.at[pl.ds(other * Z + groups * k, groups)], rc.at[pl.ds(groups * k, groups)],
            core_s, core_r, dc=1,
        )

    @pl.loop(0, n_chunks - 1)
    def _(k):
        range_chunk(lax.rem(other * half + k, n_chunks))

    pl.semaphore_wait(barrier, len(peers))
    for k in range(half):
        core_copy(k).start()
    range_chunk(c * half + half - 1)

    krows = kk // XL
    mine = pl.ds(pl.multiple_of(xl * krows, krows), krows)
    theirs = pl.ds(pl.multiple_of(xo * krows, krows), krows)

    whole(rc, core_s, core_r).wait_recv()
    for i in range(Z):
        rp[c * Z + i] = rp[c * Z + i] + rc[i]

    def z_copy(n):
        i, k = ROUND[n]
        rows_ = theirs if k else mine
        return remote(rp.at[c * Z + lax.rem(z + i, Z), rows_], rz.at[n], z_s, z_r, dz=i, dxl=k)

    for n in range(len(ROUND)):
        z_copy(n).start()

    loads[1].wait()
    loads[2].wait()
    c_rows, m_rows = a.shape[0], l.shape[0]
    rows = c_rows + m_rows
    high, low = split(a[...])
    al[:c_rows, :] = high
    al[rows : rows + c_rows, :] = low
    high, low = split(l[...])
    al[c_rows:rows, :] = high
    al[rows + c_rows :, :] = low
    loads[3].wait()
    high, low = split(q[...])
    qh[...] = high
    ql[...] = low

    piece = c_rows // (XH * Y)

    def cy_copy(dy, j):
        return remote(cp.at[j, lax.rem(y + dy, Y)], cy.at[j, dy - 1], cy_s, cy_r.at[j], dy=dy)

    def cx_copy(j):
        return remote(cs.at[j, lax.rem(xh + 1, XH)], cx.at[j], cx_s.at[j], cx_r.at[j], dxh=1)

    n_cols = fh.shape[0]

    @pl.loop(0, n_cols)
    def _(j):
        both = dot(al[...], fh[j], NN)
        out = both[:rows] + both[rows:] + dot(al[:rows, :], fl[j], NN)
        for i in range(XH):
            for k in range(Y):
                n = i * Y + k
                cp[j, k, i] = out[n * piece : (n + 1) * piece]
        high, low = split(out[c_rows:])
        mh[j] = high
        ml[j] = low
        for dy in RING:
            cy_copy(dy, j).start()

    total = None
    for j in range(n_cols):
        cols = slice(j * WIDTH, (j + 1) * WIDTH)
        part = dot(mh[j], qh[:, cols], NT) + dot(ml[j], qh[:, cols], NT) + dot(mh[j], ql[:, cols], NT)
        total = part if total is None else total + part

    trows = m_rows // (XH * Y)
    for i in range(XH * Y):
        for k in range(XL):
            mp[i, k] = total[i * trows : (i + 1) * trows, k * 128 : (k + 1) * 128]

    def ma_copy(n):
        i, j, k = PLANE[n]
        to = lax.rem(xh + i, XH) * Y + lax.rem(y + j, Y)
        return remote(mp.at[to, lax.rem(xl + k, XL)], ma.at[n], ma_s, ma_r, dxh=i, dy=j, dxl=k)

    for n in range(len(PLANE)):
        ma_copy(n).start()

    def pass_on(j):
        whole(cy.at[j], cy_s, cy_r.at[j]).wait_recv()
        cs[j] = cp[j, y] + cy[j, 0] + cy[j, 1] + cy[j, 2]
        cx_copy(j).start()

    for j in range(n_cols - 1):
        pass_on(j)

    whole(rz, z_s, z_r).wait_recv()
    done = rp[c * Z + z, mine]
    for n in range(len(ROUND)):
        done = done + rz[n]

    def spot(cc, zz, rows_):
        return range_ref.at[rows_, pl.ds(pl.multiple_of((cc * Z + zz) * 128, 128), 128)]

    own_piece = spot(c, z, mine)
    own_piece[...] = done

    def ag_copy(d):
        return remote(own_piece, own_piece, ag_s, ag_r.at[d - 1], dz=d)

    def ag_arrival(d):
        there = spot(c, lax.rem(z + Z - d, Z), mine)
        return remote(there, there, ag_s, ag_r.at[d - 1], dz=d)

    def xg_copy(d):
        there = spot(c, lax.rem(z + Z - d, Z), mine)
        return remote(there, there, xg_s, xg_r.at[d], dxl=1)

    def xg_arrival(d):
        there = spot(c, lax.rem(z + Z - d, Z), theirs)
        return remote(there, there, xg_s, xg_r.at[d], dxl=1)

    def cg_copy(d, k):
        there = spot(c, lax.rem(z + Z - d, Z), (mine, theirs)[k])
        return remote(there, there, cg_s, cg_r, dc=1)

    for d in (4, 3, 5, 2, 6, 1, 7):
        ag_copy(d).start()
    xg_copy(0).start()
    cg_copy(0, 0).start()

    def forward(order):
        for d in order:
            ag_arrival(d).wait_recv()
            xg_copy(d).start()
            cg_copy(d, 0).start()

    pass_on(n_cols - 1)

    whole(ma, ma_s, ma_r).wait_recv()
    part = mp[s, xl]
    for n in range(len(PLANE)):
        part = part + ma[n]
    part = jnp.concatenate([part, jnp.zeros((128 - trows, 128), F32)], 0).T
    for i in range(Z * C):
        mb[i] = part[8 * i : 8 * i + 8]

    def mb_copy(n):
        i, j = COLUMN[n]
        to = lax.rem(z + i, Z) * C + lax.rem(c + j, C)
        return remote(mb.at[to], mc.at[n], mb_s, mb_r, dz=i, dc=j)

    for n in range(len(COLUMN)):
        mb_copy(n).start()

    forward((1, 7, 2, 6, 3, 5, 4))
    arrivals = (0, 1, 7, 2, 6, 3, 5, 4)
    for d in arrivals:
        xg_arrival(d).wait_recv()
        cg_copy(d, 1).start()

    for j in range(n_cols):
        cx_copy(j).wait_recv()
        corange_ref[:, j * WIDTH : (j + 1) * WIDTH] = cs[j, xh] + cx[j]

    whole(mc, mb_s, mb_r).wait_recv()
    out = mb[z * C + c]
    for n in range(len(COLUMN)):
        out = out + mc[n]
    core_ref[...] = out[:, :trows]

    whole(rc, cg_s, cg_r).wait_recv()

    whole(rc, core_s, core_r).wait_send()
    whole(rz, z_s, z_r).wait_send()
    whole(rz.at[pl.ds(0, Z - 1)], ag_s, ag_r.at[0]).wait_send()
    whole(rc.at[:, mine], xg_s, xg_r.at[0]).wait_send()
    whole(rc, cg_s, cg_r).wait_send()
    whole(ma, ma_s, ma_r).wait_send()
    whole(mc, mb_s, mb_r).wait_send()
    whole(cy, cy_s, cy_r.at[0]).wait_send()
    for j in range(n_cols):
        cx_copy(j).wait_send()


def store(*refs):
    half = len(refs) // 2
    sems = refs[-1]
    copies = [pltpu.make_async_copy(refs[i], refs[half + i], sems.at[i]) for i in range(half)]
    for copy in copies:
        copy.start()
    for copy in copies:
        copy.wait()


def shards(fields, range_test, corange_test, core_left, core_right):
    cells, snaps = fields.shape
    k, l, m = range_test.shape[1], corange_test.shape[0], core_left.shape[0]
    n_cols = snaps // WIDTH
    vmem = pl.BlockSpec(memory_space=pltpu.VMEM)
    hbm = pl.BlockSpec(memory_space=pltpu.HBM)
    dma = pltpu.SemaphoreType.DMA
    v = pltpu.VMEM
    outs = (
        jax.ShapeDtypeStruct((k, cells), F32),
        jax.ShapeDtypeStruct((l // (XH * Y), snaps), F32),
        jax.ShapeDtypeStruct((m // (XL * Z * C), m // (XH * Y)), F32),
    )
    results = pl.pallas_call(
        kernel,
        out_shape=outs,
        in_specs=[hbm] * 5,
        out_specs=(vmem,) * 3,
        scratch_shapes=[
            v((cells // CHUNK, CHUNK, snaps), F32),
            v((k, snaps), F32),
            v((l, cells), F32),
            v((m, cells), F32),
            v((m, snaps), F32),
            v((n_cols, cells, WIDTH), BF16),
            v((n_cols, cells, WIDTH), BF16),
            v((2 * k, snaps), BF16),
            v((2 * (l + m), cells), BF16),
            v((m, snaps), BF16),
            v((m, snaps), BF16),
            v((n_cols, m, WIDTH), BF16),
            v((n_cols, m, WIDTH), BF16),
            v((Z * C, k, 128), F32),
            v((Z, k, 128), F32),
            v((len(ROUND), k // XL, 128), F32),
            v((n_cols, Y, XH, l // (XH * Y), WIDTH), F32),
            v((n_cols, Y - 1, XH, l // (XH * Y), WIDTH), F32),
            v((n_cols, XH, l // (XH * Y), WIDTH), F32),
            v((n_cols, l // (XH * Y), WIDTH), F32),
            v((XH * Y, XL, m // (XH * Y), 128), F32),
            v((len(PLANE), m // (XH * Y), 128), F32),
            v((Z * C, 8, 128), F32),
            v((len(COLUMN), 8, 128), F32),
            dma((cells // CHUNK,)),
            dma((4,)),
            dma, dma,
            dma, dma,
            dma, dma((Z - 1,)),
            dma, dma((Z,)),
            dma, dma,
            dma, dma((n_cols,)),
            dma((n_cols,)), dma((n_cols,)),
            dma, dma,
            dma, dma,
        ],
        compiler_params=pltpu.CompilerParams(
            collective_id=0, has_side_effects=True, vmem_limit_bytes=48 << 20
        ),
        name="sketch",
    )(*(
        pltpu.with_memory_space_constraint(x, pltpu.HBM)
        for x in (fields, range_test.T, corange_test, core_left, core_right)
    ))
    range_t, corange, core_t = pl.pallas_call(
        store,
        out_shape=outs,
        in_specs=[pl.BlockSpec(memory_space=pl.ANY)] * 3,
        out_specs=(hbm,) * 3,
        scratch_shapes=[dma((3,))],
        name="store",
    )(*(pltpu.with_memory_space_constraint(x, pltpu.VMEM) for x in results))
    return range_t.T, corange, core_t.T


def solution(mesh):
    placed = (P("space", "tm"), P("tm", None), P(None, "space"), P(None, "space"), P(None, "tm"))
    return jax.shard_map(
        shards,
        mesh=mesh,
        in_specs=placed,
        out_specs=(P("space", None), P("space", "tm"), P("space", "tm")),
        check_vma=False,
    )
```

```python
import jax
import jax.numpy as jnp
from jax import lax
from jax.experimental import pallas as pl
from jax.experimental.pallas import tpu as pltpu
from jax.sharding import PartitionSpec as P

MESH = pl.DeviceIdType.MESH
F32, BF16 = jnp.float32, jnp.bfloat16
NN = (((1,), (0,)), ((), ()))
NT = (((1,), (1,)), ((), ()))
XH, Y, XL, Z, C = 2, 4, 2, 8, 2
CHUNK = 512
WIDTH = 256
PLANE = sorted(
    ((i, j, k) for i in range(XH) for j in range(Y) for k in range(XL) if i or j or k),
    key=lambda p: (-2 * p[0] - min(p[1], Y - p[1]) - p[2], p),
)
COLUMN = sorted(
    ((i, j) for i in range(Z) for j in range(C) if i or j), key=lambda p: (-min(p[0], Z - p[0]), p)
)
ROUND = sorted(
    ((i, k) for i in range(Z) for k in range(XL) if i or k), key=lambda p: (-min(p[0], Z - p[0]) - p[1], p)
)
RING = (2, 1, 3)


def dot(a, b, dims):
    return lax.dot_general(a, b, dims, preferred_element_type=F32)


def split(x):
    high = x.astype(BF16)
    return high, (x - high.astype(F32)).astype(BF16)


def kernel(
    f_hbm, r_hbm, a_hbm, l_hbm, q_hbm,
    range_ref, corange_ref, core_ref,
    f, r, a, l, q, fh, fl, rr, al, qh, ql, mh, ml,
    rp, rc, rz, cp, cy, cs, cx, mp, ma, mb, mc,
    load_f, load, core_s, core_r, z_s, z_r, ag_s, ag_r, xg_s, xg_r, cg_s, cg_r,
    cy_s, cy_r, cx_s, cx_r, ma_s, ma_r, mb_s, mb_r,
):
    s, t = lax.axis_index("space"), lax.axis_index("tm")
    xh, y = s // Y, s % Y
    xl, z, c = t // (Z * C), (t // C) % Z, t % C

    def at(dxh=0, dy=0, dxl=0, dz=0, dc=0):
        return (
            lax.rem(xh + dxh, XH) * Y + lax.rem(y + dy, Y),
            lax.rem(xl + dxl, XL) * (Z * C) + lax.rem(z + dz, Z) * C + lax.rem(c + dc, C),
        )

    def remote(src, dst, ss, rs_, **where):
        return pltpu.make_async_remote_copy(
            src_ref=src, dst_ref=dst, send_sem=ss, recv_sem=rs_, device_id=at(**where), device_id_type=MESH
        )

    def whole(ref, ss, rs_):
        return remote(ref, ref, ss, rs_, dc=1)

    n_chunks = f.shape[0]
    half = n_chunks // C
    groups = CHUNK // 128
    other = lax.rem(c + 1, C)
    xo = lax.rem(xl + 1, XL)

    loads = [
        pltpu.make_async_copy(src, dst, load.at[i])
        for i, (src, dst) in enumerate(((r_hbm, r), (l_hbm, l), (a_hbm, a), (q_hbm, q)))
    ]

    def f_load(chunk):
        rows = pl.ds(pl.multiple_of(chunk * CHUNK, CHUNK), CHUNK)
        return pltpu.make_async_copy(f_hbm.at[rows, :], f.at[chunk], load_f.at[chunk])

    loads[0].start()
    for k in range(half):
        f_load(other * half + k).start()
    for k in range(half):
        f_load(c * half + k).start()
    for cp_ in loads[1:]:
        cp_.start()

    barrier = pltpu.get_barrier_semaphore()
    peers = {(i, j, k, 0, 0) for i, j, k in PLANE} | {(0, 0, 0, i, j) for i, j in COLUMN}
    peers |= {(0, 0, k, i, 0) for i, k in ROUND}

    def far(p):
        return -(2 * p[0] + min(p[1], Y - p[1]) + p[2] + min(p[3], Z - p[3])), p

    for i, j, k, m, n in sorted(peers, key=far):
        pl.semaphore_signal(
            barrier, inc=1, device_id=at(dxh=i, dy=j, dxl=k, dz=m, dc=n), device_id_type=MESH
        )

    loads[0].wait()
    high, low = split(r[...])
    kk = high.shape[0]
    rr[:kk, :] = high
    rr[kk:, :] = low

    def range_chunk(chunk):
        f_load(chunk).wait()
        high, low = split(f[chunk])
        rows = pl.ds(pl.multiple_of(chunk * CHUNK, CHUNK), CHUNK)
        for j in range(fh.shape[0]):
            fh[j, rows, :] = high[:, j * WIDTH : (j + 1) * WIDTH]
            fl[j, rows, :] = low[:, j * WIDTH : (j + 1) * WIDTH]
        both = dot(rr[...], high, NT)
        out = both[:kk] + both[kk:] + dot(rr[:kk, :], low, NT)
        for i in range(groups):
            rp[groups * chunk + i] = out[:, 128 * i : 128 * (i + 1)]

    def core_copy(k):
        return remote(
            rp.at[pl.ds(other * Z + groups * k, groups)], rc.at[pl.ds(groups * k, groups)],
            core_s, core_r, dc=1,
        )

    @pl.loop(0, n_chunks - 1)
    def _(k):
        range_chunk(lax.rem(other * half + k, n_chunks))

    pl.semaphore_wait(barrier, len(peers))
    for k in range(half):
        core_copy(k).start()
    range_chunk(c * half + half - 1)

    krows = kk // XL
    mine = pl.ds(pl.multiple_of(xl * krows, krows), krows)
    theirs = pl.ds(pl.multiple_of(xo * krows, krows), krows)

    whole(rc, core_s, core_r).wait_recv()
    for i in range(Z):
        rp[c * Z + i] = rp[c * Z + i] + rc[i]

    def z_copy(n):
        i, k = ROUND[n]
        rows_ = theirs if k else mine
        return remote(rp.at[c * Z + lax.rem(z + i, Z), rows_], rz.at[n], z_s, z_r, dz=i, dxl=k)

    for n in range(len(ROUND)):
        z_copy(n).start()

    loads[1].wait()
    loads[2].wait()
    c_rows, m_rows = a.shape[0], l.shape[0]
    rows = c_rows + m_rows
    high, low = split(a[...])
    al[:c_rows, :] = high
    al[rows : rows + c_rows, :] = low
    high, low = split(l[...])
    al[c_rows:rows, :] = high
    al[rows + c_rows :, :] = low
    loads[3].wait()

    piece = c_rows // (XH * Y)

    def cy_copy(dy, j):
        return remote(cp.at[j, lax.rem(y + dy, Y)], cy.at[j, dy - 1], cy_s, cy_r.at[j], dy=dy)

    def cx_copy(j):
        return remote(cs.at[j, lax.rem(xh + 1, XH)], cx.at[j], cx_s.at[j], cx_r.at[j], dxh=1)

    n_cols = fh.shape[0]

    @pl.loop(0, n_cols)
    def _(j):
        both = dot(al[...], fh[j], NN)
        out = both[:rows] + both[rows:] + dot(al[:rows, :], fl[j], NN)
        for i in range(XH):
            for k in range(Y):
                n = i * Y + k
                cp[j, k, i] = out[n * piece : (n + 1) * piece]
        high, low = split(out[c_rows:])
        mh[j] = high
        ml[j] = low
        cols = pl.ds(pl.multiple_of(j * WIDTH, WIDTH), WIDTH)
        high, low = split(q[:, cols])
        qh[:, cols] = high
        ql[:, cols] = low

        @pl.when(j < n_cols - 1)
        def _():
            for dy in RING:
                cy_copy(dy, j).start()

    total = None
    for j in range(n_cols):
        cols = slice(j * WIDTH, (j + 1) * WIDTH)
        part = dot(mh[j], qh[:, cols], NT) + dot(ml[j], qh[:, cols], NT) + dot(mh[j], ql[:, cols], NT)
        total = part if total is None else total + part

    trows = m_rows // (XH * Y)
    for i in range(XH * Y):
        for k in range(XL):
            mp[i, k] = total[i * trows : (i + 1) * trows, k * 128 : (k + 1) * 128]

    def ma_copy(n):
        i, j, k = PLANE[n]
        to = lax.rem(xh + i, XH) * Y + lax.rem(y + j, Y)
        return remote(mp.at[to, lax.rem(xl + k, XL)], ma.at[n], ma_s, ma_r, dxh=i, dy=j, dxl=k)

    for n in range(len(PLANE)):
        ma_copy(n).start()
    for dy in RING:
        cy_copy(dy, n_cols - 1).start()

    def pass_on(j):
        whole(cy.at[j], cy_s, cy_r.at[j]).wait_recv()
        cs[j] = cp[j, y] + cy[j, 0] + cy[j, 1] + cy[j, 2]
        cx_copy(j).start()

    whole(rz, z_s, z_r).wait_recv()
    done = rp[c * Z + z, mine]
    for n in range(len(ROUND)):
        done = done + rz[n]

    def spot(cc, zz, rows_):
        return range_ref.at[rows_, pl.ds(pl.multiple_of((cc * Z + zz) * 128, 128), 128)]

    own_piece = spot(c, z, mine)
    own_piece[...] = done

    def ag_copy(d):
        return remote(own_piece, own_piece, ag_s, ag_r.at[d - 1], dz=d)

    def ag_arrival(d):
        there = spot(c, lax.rem(z + Z - d, Z), mine)
        return remote(there, there, ag_s, ag_r.at[d - 1], dz=d)

    def xg_copy(d):
        there = spot(c, lax.rem(z + Z - d, Z), mine)
        return remote(there, there, xg_s, xg_r.at[d], dxl=1)

    def xg_arrival(d):
        there = spot(c, lax.rem(z + Z - d, Z), theirs)
        return remote(there, there, xg_s, xg_r.at[d], dxl=1)

    def cg_copy(d, k):
        there = spot(c, lax.rem(z + Z - d, Z), (mine, theirs)[k])
        return remote(there, there, cg_s, cg_r, dc=1)

    for d in (4, 3, 5, 2, 6, 1, 7):
        ag_copy(d).start()
    xg_copy(0).start()
    cg_copy(0, 0).start()

    def forward(order):
        for d in order:
            ag_arrival(d).wait_recv()
            xg_copy(d).start()
            cg_copy(d, 0).start()


    whole(ma, ma_s, ma_r).wait_recv()
    part = mp[s, xl]
    for n in range(len(PLANE)):
        part = part + ma[n]
    part = jnp.concatenate([part, jnp.zeros((128 - trows, 128), F32)], 0).T
    for i in range(Z * C):
        mb[i] = part[8 * i : 8 * i + 8]

    def mb_copy(n):
        i, j = COLUMN[n]
        to = lax.rem(z + i, Z) * C + lax.rem(c + j, C)
        return remote(mb.at[to], mc.at[n], mb_s, mb_r, dz=i, dc=j)

    for n in range(len(COLUMN)):
        mb_copy(n).start()

    forward((1, 7, 2, 6))
    for j in range(n_cols):
        pass_on(j)
    forward((3, 5, 4))
    arrivals = (0, 1, 7, 2, 6, 3, 5, 4)
    for d in arrivals:
        xg_arrival(d).wait_recv()
        cg_copy(d, 1).start()

    for j in range(n_cols):
        cx_copy(j).wait_recv()
        corange_ref[:, j * WIDTH : (j + 1) * WIDTH] = cs[j, xh] + cx[j]

    whole(mc, mb_s, mb_r).wait_recv()
    out = mb[z * C + c]
    for n in range(len(COLUMN)):
        out = out + mc[n]
    core_ref[...] = out[:, :trows]

    whole(rc, cg_s, cg_r).wait_recv()

    whole(rc, core_s, core_r).wait_send()
    whole(rz, z_s, z_r).wait_send()
    whole(rz.at[pl.ds(0, Z - 1)], ag_s, ag_r.at[0]).wait_send()
    whole(rc.at[:, mine], xg_s, xg_r.at[0]).wait_send()
    whole(rc, cg_s, cg_r).wait_send()
    whole(ma, ma_s, ma_r).wait_send()
    whole(mc, mb_s, mb_r).wait_send()
    whole(cy, cy_s, cy_r.at[0]).wait_send()
    for j in range(n_cols):
        cx_copy(j).wait_send()


def store(*refs):
    half = len(refs) // 2
    sems = refs[-1]
    copies = [pltpu.make_async_copy(refs[i], refs[half + i], sems.at[i]) for i in range(half)]
    for copy in copies:
        copy.start()
    for copy in copies:
        copy.wait()


def shards(fields, range_test, corange_test, core_left, core_right):
    cells, snaps = fields.shape
    k, l, m = range_test.shape[1], corange_test.shape[0], core_left.shape[0]
    n_cols = snaps // WIDTH
    vmem = pl.BlockSpec(memory_space=pltpu.VMEM)
    hbm = pl.BlockSpec(memory_space=pltpu.HBM)
    dma = pltpu.SemaphoreType.DMA
    v = pltpu.VMEM
    outs = (
        jax.ShapeDtypeStruct((k, cells), F32),
        jax.ShapeDtypeStruct((l // (XH * Y), snaps), F32),
        jax.ShapeDtypeStruct((m // (XL * Z * C), m // (XH * Y)), F32),
    )
    results = pl.pallas_call(
        kernel,
        out_shape=outs,
        in_specs=[hbm] * 5,
        out_specs=(vmem,) * 3,
        scratch_shapes=[
            v((cells // CHUNK, CHUNK, snaps), F32),
            v((k, snaps), F32),
            v((l, cells), F32),
            v((m, cells), F32),
            v((m, snaps), F32),
            v((n_cols, cells, WIDTH), BF16),
            v((n_cols, cells, WIDTH), BF16),
            v((2 * k, snaps), BF16),
            v((2 * (l + m), cells), BF16),
            v((m, snaps), BF16),
            v((m, snaps), BF16),
            v((n_cols, m, WIDTH), BF16),
            v((n_cols, m, WIDTH), BF16),
            v((Z * C, k, 128), F32),
            v((Z, k, 128), F32),
            v((len(ROUND), k // XL, 128), F32),
            v((n_cols, Y, XH, l // (XH * Y), WIDTH), F32),
            v((n_cols, Y - 1, XH, l // (XH * Y), WIDTH), F32),
            v((n_cols, XH, l // (XH * Y), WIDTH), F32),
            v((n_cols, l // (XH * Y), WIDTH), F32),
            v((XH * Y, XL, m // (XH * Y), 128), F32),
            v((len(PLANE), m // (XH * Y), 128), F32),
            v((Z * C, 8, 128), F32),
            v((len(COLUMN), 8, 128), F32),
            dma((cells // CHUNK,)),
            dma((4,)),
            dma, dma,
            dma, dma,
            dma, dma((Z - 1,)),
            dma, dma((Z,)),
            dma, dma,
            dma, dma((n_cols,)),
            dma((n_cols,)), dma((n_cols,)),
            dma, dma,
            dma, dma,
        ],
        compiler_params=pltpu.CompilerParams(
            collective_id=0, has_side_effects=True, vmem_limit_bytes=48 << 20
        ),
        name="sketch",
    )(*(
        pltpu.with_memory_space_constraint(x, pltpu.HBM)
        for x in (fields, range_test.T, corange_test, core_left, core_right)
    ))
    range_t, corange, core_t = pl.pallas_call(
        store,
        out_shape=outs,
        in_specs=[pl.BlockSpec(memory_space=pl.ANY)] * 3,
        out_specs=(hbm,) * 3,
        scratch_shapes=[dma((3,))],
        name="store",
    )(*(pltpu.with_memory_space_constraint(x, pltpu.VMEM) for x in results))
    return range_t.T, corange, core_t.T


def solution(mesh):
    placed = (P("space", "tm"), P("tm", None), P(None, "space"), P(None, "space"), P(None, "tm"))
    return jax.shard_map(
        shards,
        mesh=mesh,
        in_specs=placed,
        out_specs=(P("space", None), P("space", "tm"), P("space", "tm")),
        check_vma=False,
    )
```
